256 devices in a mesh: docs: 32 (over x, y, core), heads: 8 (over z).
Axes of the slice: x: 4, y: 4, z: 8, core: 2. Of those that a mesh axis runs over, the one named last changes fastest.
Arguments:
- queries: bfloat16 [96, 128, 8192], P('docs', 'heads'), may hold values from -12 to 12
- keys: bfloat16 [96, 128, 1024], P('docs', 'heads'), may hold values from -6 to 6
- values: bfloat16 [96, 128, 1024], P('docs', 'heads'), may hold values from -6 to 6
- out_grad: bfloat16 [96, 128, 8192], P('docs', 'heads'), may hold values from -6 to 6
- doc_keys: bfloat16 [256, 256, 1024], P('docs', None, 'heads'), may hold values from -6 to 6
- doc_values: bfloat16 [256, 256, 1024], P('docs', None, 'heads'), may hold values from -6 to 6
- owner_pick: int32 [96, 8], P('docs'), may hold values from 0 to 31, all different within a row; in each aligned block of 3 rows (0 to 2, 3 to 5, ...) at most 2 rows name the same one
- doc_pick: int32 [96, 8], P('docs'), may hold values from 0 to 7
Outputs:
- attended: bfloat16 [96, 128, 8192], P('docs', 'heads')
- query_grad: bfloat16 [96, 128, 8192], P('docs', 'heads')
- key_grad: bfloat16 [96, 128, 1024], P('docs', 'heads')
- value_grad: bfloat16 [96, 128, 1024], P('docs', 'heads')
- doc_key_grad: bfloat16 [256, 256, 1024], P('docs', None, 'heads')
- doc_value_grad: bfloat16 [256, 256, 1024], P('docs', None, 'heads')
The draws below stay inside these ranges and needn't reach their ends.
Inputs may be any that keep to these rules, and one draw needn't show every extreme that they name: `owner_pick`: each row names 8 different owners. Among the 3 rows of one index of docs no owner is named more than 2 times, a bound that some block reaches.
All inputs are finite; a program needn't handle non-finite values.
Results may differ from the reference program's by a relative error of at most 0.039.
Values may be sent and summed in bfloat16 or wider, within the bound.
No kernel may reach another device: no remote copies, remote signals or barrier semaphores. Data moves between devices by JAX's collectives and lax.ppermute only.
A program may use at most 128 MiB of HBM per device.

```python
import math
import jax
import jax.numpy as jnp
import numpy as np
from jax import lax

HD = 128
QH = 8
DLEN = 256
QLEN = 128
FAN = 8
DOC_DEV = 8
Q_DEV = 3
KVH = 8
QHEADS = 64
DOCS = 256
QBLOCKS = 96
CAP = 2
N_DOCS = 32


def draw_queries(key, part):
    key = jax.random.fold_in(key, 7)
    shape = (QBLOCKS, QLEN, KVH, QH, HD)
    base = jnp.clip(jax.random.normal(key, shape, jnp.float32), -6.0, 6.0)
    return base.reshape(QBLOCKS, QLEN, KVH * QH * HD).astype(jnp.bfloat16)


def draw_keys(key, part):
    key = jax.random.fold_in(key, 13)
    shape = (QBLOCKS, QLEN, KVH, HD)
    base = jnp.clip(jax.random.normal(key, shape, jnp.float32), -6.0, 6.0)
    return base.reshape(QBLOCKS, QLEN, KVH * HD).astype(jnp.bfloat16)


def plant(array, key, smallest, high):
    index_at = [jax.random.randint(jax.random.fold_in(key, axis), (), 0, length) for axis, length in enumerate(array.shape)]
    main_axis = array.shape.index(max(array.shape))
    beside = index_at[:main_axis] + [(index_at[main_axis] + 1) % array.shape[main_axis]] + index_at[main_axis + 1:]
    return array.at[tuple(index_at)].set(smallest).at[tuple(beside)].set(high)


def block_scale(own_key, dims, shards, low, high):
    loudness = 1.0
    for axis_at, blocks in shards:
        heights = jax.random.uniform(jax.random.fold_in(jax.random.fold_in(own_key, 6), axis_at), (blocks,), jnp.float32, low / len(shards), high / len(shards))
        loudness = loudness * jnp.repeat(jnp.exp(heights), dims[axis_at] // blocks).reshape((-1,) + (1,) * (len(dims) - 1 - axis_at))
    return loudness


def routed_block(key, own, number, rows, number_of, top, most, slope):
    order = jax.random.permutation(key, number_of)
    crowded, common = portions_of(number_of, rows * top, most, slope, True), portions_of(number_of, rows * top, most, slope, False)
    places = jnp.arange(number_of)

    def named(sizes, rotation):
        used = int((sizes > 0).sum())
        fixed = max(1, used // 4)
        passed = fixed + (places - fixed + rotation * (used - fixed)) % max(1, number_of - fixed)
        return jnp.zeros((number_of,), jnp.int32).at[order[jnp.where(places < fixed, places, passed)]].set(jnp.asarray(sizes, jnp.int32))

    sizes = jnp.where(number % 4 == 0, named(crowded, number // 4), named(common, number - number // 4 - 1))
    mixed = jax.random.permutation(jax.random.fold_in(own, 3), number_of)
    donor, sink = mixed[0:number_of // 2 * 2:2], mixed[1:number_of // 2 * 2:2]
    margin = jnp.minimum(sizes[donor] - 1, most - sizes[sink]) // 2
    margin = jnp.where((donor == order[0]) | (sink == order[0]) | (sizes[sink] == 0), 0, jnp.maximum(margin, 0))
    passed = jax.random.randint(jax.random.fold_in(own, 4), (number_of // 2,), 0, 1 << 20) % (margin + 1)
    sizes = sizes.at[donor].add(-passed).at[sink].add(passed)
    members = jnp.searchsorted(jnp.cumsum(sizes), jnp.arange(rows * top), side="right").astype(jnp.int32)
    table = members.reshape(top, rows).T
    table = table[jax.random.permutation(jax.random.fold_in(own, 1), rows)]
    rotation = jax.random.randint(jax.random.fold_in(own, 2), (rows, 1), 0, top)
    return jnp.take_along_axis(table, (jnp.arange(top)[None, :] + rotation) % top, axis=1)


def portions_of(amount, total, bound, skew, full):
    loads = [(1 << 20) // math.isqrt(rank ** skew) + 1 for rank in range(1, amount + 1)]
    largest = bound if full else min(bound, max(-(-total // amount), total * loads[0] // sum(loads)))
    least = 1 if total - largest >= amount - 1 else 0
    given, surplus = [largest] + [least] * (amount - 1), total - largest - least * (amount - 1)
    while surplus > 0:
        movable = [i for i in range(1, amount) if given[i] < largest] or [i for i in range(1, amount) if given[i] < bound]
        mass, budget = sum([loads[i] for i in movable]), surplus
        for i in movable:
            more = min(bound - given[i], max(1, budget * loads[i] // mass), surplus)
            given[i] = given[i] + more
            surplus = surplus - more
    return np.array(given)


def bell_draw(own_key, dims, deviation, bound, cuts=(), dtype=jnp.bfloat16):
    result = jax.random.normal(own_key, dims, jnp.float32) * deviation
    if len(cuts) > 0:
        result = block_scale(own_key, dims, cuts, -0.22, 0.18) * result
    return jnp.clip(result, min=-bound, max=bound).astype(dtype)


def setup_inputs(seed: int = 0) -> dict:
    seeds = jax.random.split(jax.random.key(seed), 9)
    queries = draw_queries(jax.random.fold_in(seeds[8], 71), 0)
    keys = draw_keys(jax.random.fold_in(seeds[8], 71), 0)
    values = bell_draw(seeds[2], (QBLOCKS, QLEN, KVH * HD), 1.0, 6.0, ((0, 32), (1, 8)))
    out_grad = bell_draw(seeds[3], (QBLOCKS, QLEN, QHEADS * HD), 1.0, 6.0, ((0, 32), (1, 8)))
    doc_keys = bell_draw(seeds[4], (DOCS, DLEN, KVH * HD), 1.0, 6.0, ((0, 32), (2, 8)))
    doc_values = bell_draw(seeds[5], (DOCS, DLEN, KVH * HD), 1.0, 6.0, ((0, 32), (2, 8)))
    owner_pick_keys = jax.random.split(jax.random.fold_in(seeds[6], 1), QBLOCKS // Q_DEV)
    owner_pick_turns = jax.random.permutation(jax.random.fold_in(seeds[6], 3), QBLOCKS // Q_DEV)
    owner_pick = jax.vmap(lambda own, number: routed_block(jax.random.fold_in(seeds[6], 2), own, number, Q_DEV, N_DOCS, FAN, CAP, 2))(owner_pick_keys, owner_pick_turns).reshape((QBLOCKS, FAN))
    doc_pick = plant(jax.random.randint(seeds[7], (QBLOCKS, FAN), 0, DOC_DEV), jax.random.fold_in(seeds[7], 1), 0, DOC_DEV - 1).astype(jnp.int32)
    return dict(queries=queries, keys=keys, values=values, out_grad=out_grad, doc_keys=doc_keys, doc_values=doc_values, owner_pick=owner_pick, doc_pick=doc_pick)


def attend_block(query, grad_out, key_all, value_all, kv_heads):
    length = query.shape[0]
    key_count = key_all.shape[0]
    head_dim = key_all.shape[1] // kv_heads
    group_size = query.shape[1] // (kv_heads * head_dim)
    scaling = 1.0 / math.sqrt(head_dim)
    query_heads = query.astype(jnp.float32).reshape(length, kv_heads, group_size, head_dim)
    grad_heads = grad_out.astype(jnp.float32).reshape(length, kv_heads, group_size, head_dim)
    key_heads = key_all.astype(jnp.float32).reshape(key_count, kv_heads, head_dim)
    value_heads = value_all.astype(jnp.float32).reshape(key_count, kv_heads, head_dim)
    scores = jnp.einsum('lhgd,khd->hglk', query_heads, key_heads) * scaling
    offset = key_count - length
    row_index = jnp.arange(length)[:, None]
    col_index = jnp.arange(key_count)[None, :]
    visible = (col_index < offset) | (col_index - offset <= row_index)
    scores = jnp.where(visible, scores, -jnp.inf)
    row_max = lax.optimization_barrier(jnp.max(scores, axis=-1, keepdims=True))
    log_total = row_max + jnp.log(lax.optimization_barrier(jnp.sum(jnp.exp(scores - row_max), axis=-1, keepdims=True)))
    weights = jnp.exp(scores - log_total)
    weights_low = weights.astype(jnp.bfloat16).astype(jnp.float32)
    attended = jnp.einsum('hglk,khd->lhgd', weights_low, value_heads).astype(jnp.bfloat16)
    row_dot = lax.optimization_barrier(jnp.sum(grad_heads * attended.astype(jnp.float32), axis=-1))
    row_dot = jnp.transpose(row_dot, (1, 2, 0))[..., None]
    value_grad = jnp.einsum('hglk,lhgd->khd', weights_low, grad_heads)
    weight_grad = jnp.einsum('lhgd,khd->hglk', grad_heads, value_heads)
    score_grad = (scaling * weights * (weight_grad - row_dot)).astype(jnp.bfloat16).astype(jnp.float32)
    query_grad = jnp.einsum('hglk,khd->lhgd', score_grad, key_heads).astype(jnp.bfloat16)
    key_grad = jnp.einsum('hglk,lhgd->khd', score_grad, query_heads)
    return (attended.reshape(length, -1), query_grad.reshape(length, -1), key_grad.reshape(key_count, -1), value_grad.reshape(key_count, -1))

def reference(queries, keys, values, out_grad, doc_keys, doc_values, owner_pick, doc_pick):
    chosen = (owner_pick * DOC_DEV + doc_pick).astype(jnp.int32)
    features = doc_keys.shape[2]
    doc_rows = FAN * DLEN

    def advance(totals, inputs):
        key_total, value_total = totals
        query, key_own, value_own, grad_out, chosen_docs = inputs
        doc_key_rows = doc_keys[chosen_docs].reshape(doc_rows, features)
        doc_value_rows = doc_values[chosen_docs].reshape(doc_rows, features)
        key_all = jnp.concatenate([doc_key_rows, key_own], axis=0)
        value_all = jnp.concatenate([doc_value_rows, value_own], axis=0)
        attended, query_grad, key_grad, value_grad = attend_block(query, grad_out, key_all, value_all, KVH)
        pair_key = lax.optimization_barrier(key_grad[:doc_rows].astype(jnp.bfloat16)).astype(jnp.float32)
        pair_value = lax.optimization_barrier(value_grad[:doc_rows].astype(jnp.bfloat16)).astype(jnp.float32)
        key_total = key_total.at[chosen_docs].add(pair_key.reshape(FAN, DLEN, features))
        value_total = value_total.at[chosen_docs].add(pair_value.reshape(FAN, DLEN, features))
        return ((key_total, value_total), (attended, query_grad, key_grad[doc_rows:].astype(jnp.bfloat16), value_grad[doc_rows:].astype(jnp.bfloat16)))
    zeros_grid = jnp.zeros((DOCS, DLEN, features), jnp.float32)
    totals, stacked = lax.scan(advance, (zeros_grid, zeros_grid), (queries, keys, values, out_grad, chosen))
    attended, query_grad, key_grad, value_grad = stacked
    return (attended, query_grad, key_grad, value_grad, totals[0].astype(jnp.bfloat16), totals[1].astype(jnp.bfloat16))
```

```python
import functools
import math

import jax
import jax.numpy as jnp
from jax import lax
from jax.experimental import pallas as pl
from jax.experimental.pallas import tpu as pltpu
from jax.sharding import PartitionSpec as P

VMEM_LIMIT = 60 * 1024 * 1024
SLICE = 16
LOG2E = 1.4426950408889634


def vmem():
    return pl.BlockSpec(memory_space=pltpu.VMEM)


def smem():
    return pl.BlockSpec(memory_space=pltpu.SMEM)


def params(**kw):
    return pltpu.CompilerParams(vmem_limit_bytes=VMEM_LIMIT, **kw)


def split_docs(doc_keys, doc_values, owner_pick, doc_pick, peers):
    docs, length, head_dim = doc_keys.shape
    blocks, fan = owner_pick.shape
    half = peers // 2

    def kernel(key_ref, value_ref, owner_ref, pick_ref, out_ref):
        chosen = (owner_ref[...] * docs + pick_ref[...]).astype(jnp.float32)
        chosen = jnp.pad(chosen, ((0, SLICE - blocks), (0, head_dim - fan)))
        chosen = chosen.astype(jnp.bfloat16)
        for i in range(half):
            rows = slice(i * SLICE, (i + 1) * SLICE)
            out_ref[i, :docs] = key_ref[:, rows, :]
            out_ref[half + i, :docs] = value_ref[:, rows, :]
            out_ref[i, docs] = chosen
            out_ref[half + i, docs] = chosen

    return pl.pallas_call(
        kernel,
        out_shape=jax.ShapeDtypeStruct((peers, docs + 1, SLICE, head_dim), jnp.bfloat16),
        in_specs=[vmem()] * 4,
        out_specs=vmem(),
        compiler_params=params(),
    )(doc_keys, doc_values, owner_pick, doc_pick)


def join_docs(slices):
    peers, docs, rows, head_dim = slices.shape
    half = peers // 2
    shape = jax.ShapeDtypeStruct((docs, half * rows, head_dim), jnp.bfloat16)

    def kernel(in_ref, key_ref, value_ref):
        for i in range(half):
            at = slice(i * rows, (i + 1) * rows)
            key_ref[:, at, :] = in_ref[i]
            value_ref[:, at, :] = in_ref[half + i]

    return pl.pallas_call(
        kernel,
        out_shape=(shape, shape),
        in_specs=[vmem()],
        out_specs=(vmem(), vmem()),
        compiler_params=params(),
    )(slices)


def split_heads(me, queries, out_grad, keys, values, peers):
    blocks, rows, features = queries.shape
    wide = features // peers
    narrow = keys.shape[2] // peers
    width = 2 * wide + 2 * narrow

    def kernel(me_ref, q_ref, g_ref, k_ref, v_ref, *outs):
        for s in range(peers):
            head = lax.rem(me_ref[0] + s, peers)
            big = pl.ds(pl.multiple_of(head * wide, wide), wide)
            small = pl.ds(pl.multiple_of(head * narrow, narrow), narrow)
            outs[s][:, :, 0:wide] = q_ref[:, :, big]
            outs[s][:, :, wide : 2 * wide] = g_ref[:, :, big]
            outs[s][:, :, 2 * wide : 2 * wide + narrow] = k_ref[:, :, small]
            outs[s][:, :, 2 * wide + narrow : width] = v_ref[:, :, small]

    shape = jax.ShapeDtypeStruct((blocks, rows, width), jnp.bfloat16)
    return pl.pallas_call(
        kernel,
        out_shape=(shape,) * peers,
        in_specs=[smem()] + [vmem()] * 4,
        out_specs=(vmem(),) * peers,
        compiler_params=params(),
    )(me, queries, out_grad, keys, values)


def join_heads(me, parts, wide, narrow):
    peers = len(parts)
    blocks, rows, width = parts[0].shape

    def kernel(me_ref, *refs):
        ins, (a_ref, q_ref, k_ref, v_ref) = refs[:peers], refs[peers:]
        for s in range(peers):
            head = lax.rem(me_ref[0] + s, peers)
            big = pl.ds(pl.multiple_of(head * wide, wide), wide)
            small = pl.ds(pl.multiple_of(head * narrow, narrow), narrow)
            a_ref[:, :, big] = ins[s][:, :, 0:wide]
            q_ref[:, :, big] = ins[s][:, :, wide : 2 * wide]
            k_ref[:, :, small] = ins[s][:, :, 2 * wide : 2 * wide + narrow]
            v_ref[:, :, small] = ins[s][:, :, 2 * wide + narrow : width]

    big_shape = jax.ShapeDtypeStruct((blocks, rows, peers * wide), jnp.bfloat16)
    small_shape = jax.ShapeDtypeStruct((blocks, rows, peers * narrow), jnp.bfloat16)
    return pl.pallas_call(
        kernel,
        out_shape=(big_shape, big_shape, small_shape, small_shape),
        in_specs=[smem()] + [vmem()] * peers,
        out_specs=(vmem(),) * 4,
        compiler_params=params(),
    )(me, *parts)


def gather_pairs(slices, blocks, fan, steps=4):
    peers, kept, rows, head_dim = slices.shape
    docs = kept - 1
    count = peers // steps
    table_shape = (peers, 8, head_dim)

    shift = docs.bit_length() - 1

    def kernel(in_ref, out_ref, table_ref, slot_ref, chosen_ref, sem):
        step = pl.program_id(0)
        flat_ref = in_ref.reshape(peers * kept, rows, head_dim)

        @pl.when(step == 0)
        def _():
            tile = in_ref[:, docs].astype(jnp.float32)
            table = tile[:, :8].astype(jnp.int32)
            table_ref[...] = table
            slot_ref[...] = table + lax.shift_right_logical(table, shift)
            copy = pltpu.make_async_copy(slot_ref, chosen_ref, sem)
            copy.start()
            copy.wait()

        def body(i, _):
            q = step * count + i
            for b in range(blocks):
                for f in range(fan):
                    out_ref[i, b * fan + f] = flat_ref[chosen_ref[q, b, f]]
            return 0

        lax.fori_loop(0, count, body, 0)

    return pl.pallas_call(
        kernel,
        out_shape=(
            jax.ShapeDtypeStruct((peers, blocks * fan, rows, head_dim), jnp.bfloat16),
            jax.ShapeDtypeStruct(table_shape, jnp.int32),
        ),
        grid=(steps,),
        in_specs=[pl.BlockSpec(slices.shape, lambda i: (0, 0, 0, 0))],
        out_specs=(
            pl.BlockSpec((count, blocks * fan, rows, head_dim), lambda i: (i, 0, 0, 0)),
            pl.BlockSpec(table_shape, lambda i: (0, 0, 0)),
        ),
        scratch_shapes=[
            pltpu.VMEM(table_shape, jnp.int32),
            pltpu.SMEM(table_shape, jnp.int32),
            pltpu.SemaphoreType.DMA,
        ],
        compiler_params=params(),
    )(slices)


def sum_pairs(table, pairs, docs, blocks, fan, steps=4):
    peers, _, rows, head_dim = pairs.shape
    count = peers // steps

    def kernel(chosen_ref, in_ref, out_ref, acc_ref):
        step = pl.program_id(0)

        @pl.when(step == 0)
        def _():
            acc_ref[...] = jnp.zeros_like(acc_ref)

        def body(i, _):
            q = step * count + i
            for b in range(blocks):
                at = [chosen_ref[q, b, f] for f in range(fan)]
                sums = [
                    acc_ref[at[f]] + in_ref[i, b * fan + f].astype(jnp.float32)
                    for f in range(fan)
                ]
                for f in range(fan):
                    acc_ref[at[f]] = sums[f]
            return 0

        lax.fori_loop(0, count, body, 0)

        @pl.when(step == steps - 1)
        def _():
            total = acc_ref[...].astype(jnp.bfloat16)
            out_ref[...] = total.reshape(out_ref.shape)

    return pl.pallas_call(
        kernel,
        out_shape=jax.ShapeDtypeStruct((peers, docs, rows, head_dim), jnp.bfloat16),
        grid=(steps,),
        in_specs=[
            smem(),
            pl.BlockSpec((count, blocks * fan, rows, head_dim), lambda i: (i, 0, 0, 0)),
        ],
        out_specs=pl.BlockSpec((peers, docs, rows, head_dim), lambda i: (0, 0, 0, 0)),
        scratch_shapes=[pltpu.VMEM((peers * docs, rows, head_dim), jnp.float32)],
        compiler_params=params(),
    )(table, pairs)


def attend_kernel(
    peers, rows, group, head_dim, me_ref, kv_ref, *refs
):
    ins, refs = refs[:peers], refs[peers:]
    dkv_ref, outs = refs[0], refs[1 : 1 + peers]
    k_all, v_all, k_t, v_t, q_n, q_t, g_n, g_t, s_t, p_t, ds_t = refs[1 + peers :]
    half, fan = kv_ref.shape[0] // 2, kv_ref.shape[1]
    doc_rows = half * fan * SLICE
    own = peers * rows
    keys_all = doc_rows + own
    wide = group * head_dim
    scaling = 1.0 / math.sqrt(head_dim)
    f32, bf16 = jnp.float32, jnp.bfloat16

    def dot(a, b):
        return jnp.dot(a, b, preferred_element_type=f32)

    k_all[:doc_rows] = kv_ref[:half].reshape(doc_rows, head_dim)
    v_all[:doc_rows] = kv_ref[half:].reshape(doc_rows, head_dim)
    for s in range(peers):
        at = slice(doc_rows + s * rows, doc_rows + (s + 1) * rows)
        k_all[at] = ins[s][0, :, 2 * wide : 2 * wide + head_dim]
        v_all[at] = ins[s][0, :, 2 * wide + head_dim : 2 * wide + 2 * head_dim]
        for g in range(group):
            to = slice(g * own + s * rows, g * own + (s + 1) * rows)
            q_n[to] = ins[s][0, :, g * head_dim : (g + 1) * head_dim]
            g_n[to] = ins[s][0, :, wide + g * head_dim : wide + (g + 1) * head_dim]
    k_t[...] = k_all[...].T
    v_t[:head_dim] = v_all[...].T
    v_t[head_dim:] = jnp.ones((v_t.shape[0] - head_dim, keys_all), bf16)
    q_t[...] = q_n[...].T
    g_t[...] = g_n[...].T

    def place(index):
        source = lax.rem(me_ref[0] + peers - index // rows, peers)
        return source * rows + lax.rem(index, rows)

    chunk = 2 * own
    key_place = place(lax.broadcasted_iota(jnp.int32, (own, chunk), 0))
    query_place = place(lax.rem(lax.broadcasted_iota(jnp.int32, (own, chunk), 1), own))
    hidden = key_place > query_place

    for c in range(group // 2):
        at = slice(c * chunk, (c + 1) * chunk)
        q_c = q_t[:, at]
        g_c = g_t[:, at]
        s_doc = dot(k_all[:doc_rows], q_c)
        s_t[:doc_rows] = s_doc
        s_own = jnp.where(hidden, -jnp.inf, dot(k_all[doc_rows:], q_c))
        s_t[doc_rows:] = s_own
        top = jnp.maximum(
            jnp.max(s_doc, axis=0, keepdims=True), jnp.max(s_own, axis=0, keepdims=True)
        )
        p = jnp.exp2((s_t[...] - top) * (scaling * LOG2E)).astype(bf16)
        p_t[:, at] = p
        o = dot(v_t[...], p)
        inverse = 1.0 / o[head_dim : head_dim + 1]
        attended = (o[:head_dim] * inverse).astype(bf16)
        row_dot = jnp.sum(
            g_c.astype(f32) * attended.astype(f32), axis=0, keepdims=True
        )
        g_n[at] = (g_c.astype(f32) * inverse).astype(bf16).T
        dp = dot(v_all[...], g_c)
        ds = (p.astype(f32) * ((dp - row_dot) * (inverse * scaling))).astype(bf16)
        ds_t[:, at] = ds
        dq = dot(k_t[...], ds).astype(bf16).T
        attended = attended.T
        for g in range(2):
            lanes = slice((2 * c + g) * head_dim, (2 * c + g + 1) * head_dim)
            shifted = slice(wide + lanes.start, wide + lanes.stop)
            for s in range(peers):
                r = slice(g * own + s * rows, g * own + (s + 1) * rows)
                outs[s][0, :, lanes] = attended[r]
                outs[s][0, :, shifted] = dq[r]

    dv = dot(p_t[...], g_n[...]).astype(bf16)
    dk = dot(ds_t[...], q_n[...]).astype(bf16)
    dkv_ref[:half] = dk[:doc_rows].reshape(half, fan, SLICE, head_dim)
    dkv_ref[half:] = dv[:doc_rows].reshape(half, fan, SLICE, head_dim)
    for s in range(peers):
        at = slice(doc_rows + s * rows, doc_rows + (s + 1) * rows)
        outs[s][0, :, 2 * wide : 2 * wide + head_dim] = dk[at]
        outs[s][0, :, 2 * wide + head_dim : 2 * wide + 2 * head_dim] = dv[at]


def attend(me, pairs, parts, group, head_dim, fan):
    peers = len(parts)
    blocks, rows, width = parts[0].shape
    relays = pairs.shape[0]
    own = peers * rows
    queries = group * own
    keys_all = relays // 2 * fan * SLICE + own
    bf16, f32 = jnp.bfloat16, jnp.float32
    part_spec = pl.BlockSpec((1, rows, width), lambda b: (b, 0, 0))
    pair_spec = pl.BlockSpec((relays, fan, SLICE, head_dim), lambda b: (0, b, 0, 0))
    part_shape = jax.ShapeDtypeStruct((blocks, rows, width), bf16)
    flops = 12 * blocks * queries * keys_all * head_dim
    return pl.pallas_call(
        functools.partial(attend_kernel, peers, rows, group, head_dim),
        out_shape=(jax.ShapeDtypeStruct(pairs.shape, bf16),) + (part_shape,) * peers,
        grid=(blocks,),
        in_specs=[smem(), pair_spec] + [part_spec] * peers,
        out_specs=(pair_spec,) + (part_spec,) * peers,
        scratch_shapes=[
            pltpu.VMEM((keys_all, head_dim), bf16),
            pltpu.VMEM((keys_all, head_dim), bf16),
            pltpu.VMEM((head_dim, keys_all), bf16),
            pltpu.VMEM((head_dim + 16, keys_all), bf16),
            pltpu.VMEM((queries, head_dim), bf16),
            pltpu.VMEM((head_dim, queries), bf16),
            pltpu.VMEM((queries, head_dim), bf16),
            pltpu.VMEM((head_dim, queries), bf16),
            pltpu.VMEM((keys_all, 2 * own), f32),
            pltpu.VMEM((keys_all, queries), bf16),
            pltpu.VMEM((keys_all, queries), bf16),
        ],
        compiler_params=params(),
        cost_estimate=pl.CostEstimate(
            flops=flops,
            bytes_accessed=2 * pairs.size * 2 + 4 * peers * parts[0].size,
            transcendentals=blocks * queries * keys_all,
        ),
    )(me, pairs, *parts)


def exchange(x):
    return lax.all_to_all(x, "docs", split_axis=0, concat_axis=0, tiled=True)


def send(x, distance, peers):
    return lax.ppermute(x, "heads", [(i, (i + distance) % peers) for i in range(peers)])


def shards(queries, keys, values, out_grad, doc_keys, doc_values, owner_pick, doc_pick):
    relays = lax.axis_size("docs")
    peers = lax.axis_size("heads")
    me = lax.axis_index("heads").astype(jnp.int32).reshape(1)
    blocks, fan = owner_pick.shape
    docs, _, head_dim = doc_keys.shape
    wide = queries.shape[2] // peers
    narrow = keys.shape[2] // peers
    group = wide // head_dim

    near, far = (1, 7, 2, 6), (3, 5, 4)
    parts = split_heads(me, queries, out_grad, keys, values, peers)
    got = {0: parts[0]}
    slices = exchange(split_docs(doc_keys, doc_values, owner_pick, doc_pick, relays))
    first = [send(parts[s], s, peers) for s in near]
    slices, *first = lax.optimization_barrier([slices] + first)
    got.update(zip(near, first))
    pairs, table = gather_pairs(slices, blocks, fan)
    pairs = exchange(pairs)
    got.update((s, send(parts[s], s, peers)) for s in far)

    parts = [got[s] for s in range(peers)]
    pair_grads, *parts = attend(me, pairs, parts, group, head_dim, fan)

    back = {0: parts[0]}
    pair_grads = exchange(pair_grads)
    near, far = (1, 7), (3, 5, 4, 2, 6)
    first = [send(parts[s], -s, peers) for s in far]
    pair_grads, *first = lax.optimization_barrier([pair_grads] + first)
    back.update(zip(far, first))
    doc_grads = exchange(sum_pairs(table, pair_grads, docs, blocks, fan))
    back.update((s, send(parts[s], -s, peers)) for s in near)
    doc_key_grad, doc_value_grad = join_docs(doc_grads)
    parts = [back[s] for s in range(peers)]
    attended, query_grad, key_grad, value_grad = join_heads(me, parts, wide, narrow)
    return (attended, query_grad, key_grad, value_grad, doc_key_grad, doc_value_grad)


def solution(mesh):
    tokens = P("docs", "heads", None)
    documents = P("docs", None, "heads")
    picks = P("docs", None)
    return jax.shard_map(
        shards,
        mesh=mesh,
        in_specs=(tokens,) * 4 + (documents,) * 2 + (picks,) * 2,
        out_specs=(tokens,) * 4 + (documents,) * 2,
        check_vma=False,
    )
```

```python
import functools
import math

import jax
import jax.numpy as jnp
from jax import lax
from jax.experimental import pallas as pl
from jax.experimental.pallas import tpu as pltpu
from jax.sharding import PartitionSpec as P

VMEM_LIMIT = 63 * 1024 * 1024
SLICE = 16
LOG2E = 1.4426950408889634


def vmem():
    return pl.BlockSpec(memory_space=pltpu.VMEM)


def smem():
    return pl.BlockSpec(memory_space=pltpu.SMEM)


def params(**kw):
    return pltpu.CompilerParams(vmem_limit_bytes=VMEM_LIMIT, **kw)


def split_docs(doc_keys, doc_values, owner_pick, doc_pick, peers):
    docs, length, head_dim = doc_keys.shape
    blocks, fan = owner_pick.shape
    half = peers // 2

    def kernel(key_ref, value_ref, owner_ref, pick_ref, out_ref):
        chosen = (owner_ref[...] * docs + pick_ref[...]).astype(jnp.float32)
        row = jnp.concatenate([chosen[b : b + 1] for b in range(blocks)], axis=1)
        row = jnp.pad(row, ((0, 0), (0, head_dim - blocks * fan)))
        chosen = jnp.broadcast_to(row, (SLICE, head_dim)).astype(jnp.bfloat16)
        for i in range(half):
            rows = slice(i * SLICE, (i + 1) * SLICE)
            out_ref[i, :docs] = key_ref[:, rows, :]
            out_ref[half + i, :docs] = value_ref[:, rows, :]
            out_ref[i, docs] = chosen
            out_ref[half + i, docs] = chosen

    return pl.pallas_call(
        kernel,
        out_shape=jax.ShapeDtypeStruct((peers, docs + 1, SLICE, head_dim), jnp.bfloat16),
        in_specs=[vmem()] * 4,
        out_specs=vmem(),
        compiler_params=params(),
    )(doc_keys, doc_values, owner_pick, doc_pick)


def join_docs(slices, steps=2):
    peers, docs, rows, head_dim = slices.shape
    half = peers // 2
    part = docs // steps
    shape = jax.ShapeDtypeStruct((docs, half * rows, head_dim), jnp.bfloat16)
    doc_spec = pl.BlockSpec((part, half * rows, head_dim), lambda i: (i, 0, 0))

    def kernel(in_ref, key_ref, value_ref):
        for i in range(half):
            at = slice(i * rows, (i + 1) * rows)
            key_ref[:, at, :] = in_ref[i]
            value_ref[:, at, :] = in_ref[half + i]

    return pl.pallas_call(
        kernel,
        out_shape=(shape, shape),
        grid=(steps,),
        in_specs=[pl.BlockSpec((peers, part, rows, head_dim), lambda i: (0, i, 0, 0))],
        out_specs=(doc_spec, doc_spec),
        compiler_params=params(),
    )(slices)


def split_heads(me, queries, out_grad, keys, values, peers):
    blocks, rows, features = queries.shape
    wide = features // peers
    narrow = keys.shape[2] // peers
    width = 2 * wide + 2 * narrow

    def kernel(me_ref, q_ref, g_ref, k_ref, v_ref, *outs):
        for s in range(peers):
            head = lax.rem(me_ref[0] + s, peers)
            big = pl.ds(pl.multiple_of(head * wide, wide), wide)
            small = pl.ds(pl.multiple_of(head * narrow, narrow), narrow)
            outs[s][:, :, 0:wide] = q_ref[:, :, big]
            outs[s][:, :, wide : 2 * wide] = g_ref[:, :, big]
            outs[s][:, :, 2 * wide : 2 * wide + narrow] = k_ref[:, :, small]
            outs[s][:, :, 2 * wide + narrow : width] = v_ref[:, :, small]

    shape = jax.ShapeDtypeStruct((blocks, rows, width), jnp.bfloat16)
    return pl.pallas_call(
        kernel,
        out_shape=(shape,) * peers,
        in_specs=[smem()] + [vmem()] * 4,
        out_specs=(vmem(),) * peers,
        compiler_params=params(),
    )(me, queries, out_grad, keys, values)


def join_heads(me, parts, wide, narrow):
    peers = len(parts)
    blocks, rows, width = parts[0].shape

    def kernel(me_ref, *refs):
        ins, (a_ref, q_ref, k_ref, v_ref) = refs[:peers], refs[peers:]
        for s in range(peers):
            head = lax.rem(me_ref[0] + s, peers)
            big = pl.ds(pl.multiple_of(head * wide, wide), wide)
            small = pl.ds(pl.multiple_of(head * narrow, narrow), narrow)
            a_ref[:, :, big] = ins[s][:, :, 0:wide]
            q_ref[:, :, big] = ins[s][:, :, wide : 2 * wide]
            k_ref[:, :, small] = ins[s][:, :, 2 * wide : 2 * wide + narrow]
            v_ref[:, :, small] = ins[s][:, :, 2 * wide + narrow : width]

    big_shape = jax.ShapeDtypeStruct((blocks, rows, peers * wide), jnp.bfloat16)
    small_shape = jax.ShapeDtypeStruct((blocks, rows, peers * narrow), jnp.bfloat16)
    return pl.pallas_call(
        kernel,
        out_shape=(big_shape, big_shape, small_shape, small_shape),
        in_specs=[smem()] + [vmem()] * peers,
        out_specs=(vmem(),) * 4,
        compiler_params=params(),
    )(me, *parts)


def gather_pairs(slices, blocks, fan, steps=2):
    peers, kept, rows, head_dim = slices.shape
    docs = kept - 1
    shift = docs.bit_length() - 1
    part = peers // steps
    pairs = blocks * fan
    table_shape = (peers, head_dim)

    def kernel(in_ref, out_ref, table_ref, chosen_ref, sem):
        step = pl.program_id(0)
        flat_ref = in_ref.reshape(peers * kept, rows, head_dim)

        @pl.when(step == 0)
        def _():
            tile = in_ref[:, docs].astype(jnp.float32)
            table = tile[:, 0].astype(jnp.int32)
            table_ref[...] = table + lax.shift_right_logical(table, shift)
            copy = pltpu.make_async_copy(table_ref, chosen_ref, sem)
            copy.start()
            copy.wait()

        def body(i, _):
            q = step * part + i
            for p in range(0, pairs, fan):
                tiles = [flat_ref[chosen_ref[q, p + f]] for f in range(fan)]
                for f in range(fan):
                    out_ref[i, p + f] = tiles[f]
            return 0

        lax.fori_loop(0, part, body, 0)

    return pl.pallas_call(
        kernel,
        out_shape=(
            jax.ShapeDtypeStruct((peers, pairs, rows, head_dim), jnp.bfloat16),
            jax.ShapeDtypeStruct(table_shape, jnp.int32),
        ),
        grid=(steps,),
        in_specs=[pl.BlockSpec(slices.shape, lambda i: (0, 0, 0, 0))],
        out_specs=(
            pl.BlockSpec((part, pairs, rows, head_dim), lambda i: (i, 0, 0, 0)),
            pl.BlockSpec(table_shape, lambda i: (0, 0)),
        ),
        scratch_shapes=[
            pltpu.SMEM(table_shape, jnp.int32),
            pltpu.SemaphoreType.DMA,
        ],
        compiler_params=params(),
    )(slices)


def sum_pairs(table, pairs, kept, fan, steps=2):
    peers, count, rows, head_dim = pairs.shape
    part = peers // steps
    out_shape = (peers, kept - 1, rows, head_dim)

    def kernel(chosen_ref, in_ref, out_ref, acc_ref):
        step = pl.program_id(0)

        @pl.when(step == 0)
        def _():
            acc_ref[...] = jnp.zeros_like(acc_ref)

        def body(i, _):
            q = step * part + i
            for p in range(0, count, fan):
                at = [chosen_ref[q, p + f] for f in range(fan)]
                sums = [
                    acc_ref[at[f]] + in_ref[i, p + f].astype(jnp.float32)
                    for f in range(fan)
                ]
                for f in range(fan):
                    acc_ref[at[f]] = sums[f]
            return 0

        lax.fori_loop(0, part, body, 0)

        @pl.when(step == steps - 1)
        def _():
            for i in range(peers):
                rounded = acc_ref[i * kept : i * kept + kept - 1]
                out_ref[i] = rounded.astype(jnp.bfloat16)

    return pl.pallas_call(
        kernel,
        out_shape=jax.ShapeDtypeStruct(out_shape, jnp.bfloat16),
        grid=(steps,),
        in_specs=[
            smem(),
            pl.BlockSpec((part, count, rows, head_dim), lambda i: (i, 0, 0, 0)),
        ],
        out_specs=pl.BlockSpec(out_shape, lambda i: (0, 0, 0, 0)),
        scratch_shapes=[pltpu.VMEM((peers * kept, rows, head_dim), jnp.float32)],
        compiler_params=params(),
    )(table, pairs)


def attend_kernel(
    peers, rows, group, head_dim, me_ref, kv_ref, *refs
):
    ins, refs = refs[:peers], refs[peers:]
    dkv_ref, outs = refs[0], refs[1 : 1 + peers]
    k_all, v_all, k_t, v_t, q_n, q_t, g_n, g_t, s_t, p_t, ds_t = refs[1 + peers :]
    half, fan = kv_ref.shape[0] // 2, kv_ref.shape[1]
    doc_rows = half * fan * SLICE
    own = peers * rows
    keys_all = doc_rows + own
    wide = group * head_dim
    scaling = 1.0 / math.sqrt(head_dim)
    f32, bf16 = jnp.float32, jnp.bfloat16
    queries = group * own

    def dot(a, b):
        return jnp.dot(a, b, preferred_element_type=f32)

    k_all[:doc_rows] = kv_ref[:half].reshape(doc_rows, head_dim)
    v_all[:doc_rows] = kv_ref[half:].reshape(doc_rows, head_dim)
    for s in range(peers):
        at = slice(doc_rows + s * rows, doc_rows + (s + 1) * rows)
        k_all[at] = ins[s][0, :, 2 * wide : 2 * wide + head_dim]
        v_all[at] = ins[s][0, :, 2 * wide + head_dim : 2 * wide + 2 * head_dim]
        for g in range(group):
            to = slice(g * own + s * rows, g * own + (s + 1) * rows)
            q_n[to] = ins[s][0, :, g * head_dim : (g + 1) * head_dim]
            g_n[to] = ins[s][0, :, wide + g * head_dim : wide + (g + 1) * head_dim]
    k_t[...] = k_all[...].T
    v_t[:head_dim] = v_all[...].T
    v_t[head_dim:] = jnp.ones((v_t.shape[0] - head_dim, keys_all), bf16)
    q_t[...] = q_n[...].T
    g_t[...] = g_n[...].T

    def place(index):
        source = lax.rem(me_ref[0] + peers - index // rows, peers)
        return source * rows + lax.rem(index, rows)

    chunk = 2 * own
    key_place = place(lax.broadcasted_iota(jnp.int32, (own, chunk), 0))
    query_place = place(lax.rem(lax.broadcasted_iota(jnp.int32, (own, chunk), 1), own))
    hidden = key_place > query_place
    tiles = [slice(t, min(t + 256, doc_rows)) for t in range(0, doc_rows, 256)]
    tiles.append(slice(doc_rows, keys_all))

    def rows_max(x):
        return jnp.max(x.reshape(x.shape[0] // 8, 8, chunk), axis=0)

    def score(c, buf):
        q_c = q_t[:, c * chunk : (c + 1) * chunk]
        top = None
        for t in tiles:
            x = dot(k_all[t], q_c)
            if t.start == doc_rows:
                x = jnp.where(hidden, -jnp.inf, x)
            buf[t] = x
            m = rows_max(x)
            top = m if top is None else jnp.maximum(top, m)
        return jnp.max(top, axis=0, keepdims=True)

    def finish(c, o):
        at = slice(c * chunk, (c + 1) * chunk)
        g_c = g_t[:, at].astype(f32)
        inverse = 1.0 / o[head_dim : head_dim + 1]
        attended = (o[:head_dim] * inverse).astype(bf16)
        row_dot = jnp.sum(g_c * attended.astype(f32), axis=0, keepdims=True)
        g_n[at] = (g_c * inverse).astype(bf16).T
        return attended, row_dot, inverse * scaling

    def put(c, x, base):
        x = x.T
        for g in range(chunk // own):
            lanes = slice(base + (c * (chunk // own) + g) * head_dim, base + (c * (chunk // own) + g + 1) * head_dim)
            for s in range(peers):
                outs[s][0, :, lanes] = x[g * own + s * rows : g * own + (s + 1) * rows]

    tops = [score(0, s_t.at[0])]
    count = queries // chunk
    for c in range(count):
        at = slice(c * chunk, (c + 1) * chunk)
        cur, nxt = s_t.at[c % 2], s_t.at[(c + 1) % 2]
        m = None
        q_c = q_t[:, (c + 1) * chunk : (c + 2) * chunk] if c + 1 < count else None
        for t in tiles:
            p_t[t, at] = jnp.exp2((cur[t] - tops[c]) * (scaling * LOG2E)).astype(bf16)
            if q_c is not None:
                x = dot(k_all[t], q_c)
                if t.start == doc_rows:
                    x = jnp.where(hidden, -jnp.inf, x)
                nxt[t] = x
                y = rows_max(x)
                m = y if m is None else jnp.maximum(m, y)
        if m is not None:
            tops.append(jnp.max(m, axis=0, keepdims=True))
        attended, row_dot, factor = finish(c, dot(v_t[...], p_t[:, at]))
        g_c = g_t[:, at]
        for t in tiles:
            dp = dot(v_all[t], g_c)
            ds_t[t, at] = (p_t[t, at].astype(f32) * ((dp - row_dot) * factor)).astype(bf16)
        put(c, attended, 0)
        put(c, dot(k_t[...], ds_t[:, at]).astype(bf16), wide)

    dv = dot(p_t[...], g_n[...]).astype(bf16)
    dk = dot(ds_t[...], q_n[...]).astype(bf16)
    dkv_ref[:half] = dk[:doc_rows].reshape(half, fan, SLICE, head_dim)
    dkv_ref[half:] = dv[:doc_rows].reshape(half, fan, SLICE, head_dim)
    for s in range(peers):
        at = slice(doc_rows + s * rows, doc_rows + (s + 1) * rows)
        outs[s][0, :, 2 * wide : 2 * wide + head_dim] = dk[at]
        outs[s][0, :, 2 * wide + head_dim : 2 * wide + 2 * head_dim] = dv[at]


def attend(me, pairs, parts, group, head_dim, fan):
    peers = len(parts)
    _, rows, width = parts[0].shape
    relays = pairs.shape[0]
    blocks = pairs.shape[1] // fan
    own = peers * rows
    queries = group * own
    keys_all = relays // 2 * fan * SLICE + own
    bf16, f32 = jnp.bfloat16, jnp.float32
    part_spec = pl.BlockSpec((1, rows, width), lambda b: (b, 0, 0))
    pair_spec = pl.BlockSpec((relays, fan, SLICE, head_dim), lambda b: (0, b, 0, 0))
    part_shape = jax.ShapeDtypeStruct(parts[0].shape, bf16)
    flops = 12 * blocks * queries * keys_all * head_dim
    return pl.pallas_call(
        functools.partial(attend_kernel, peers, rows, group, head_dim),
        out_shape=(jax.ShapeDtypeStruct(pairs.shape, bf16),) + (part_shape,) * peers,
        grid=(blocks,),
        in_specs=[smem(), pair_spec] + [part_spec] * peers,
        out_specs=(pair_spec,) + (part_spec,) * peers,
        scratch_shapes=[
            pltpu.VMEM((keys_all, head_dim), bf16),
            pltpu.VMEM((keys_all, head_dim), bf16),
            pltpu.VMEM((head_dim, keys_all), bf16),
            pltpu.VMEM((head_dim + 16, keys_all), bf16),
            pltpu.VMEM((queries, head_dim), bf16),
            pltpu.VMEM((head_dim, queries), bf16),
            pltpu.VMEM((queries, head_dim), bf16),
            pltpu.VMEM((head_dim, queries), bf16),
            pltpu.VMEM((2, keys_all, 2 * own), f32),
            pltpu.VMEM((keys_all, queries), bf16),
            pltpu.VMEM((keys_all, queries), bf16),
        ],
        compiler_params=params(),
        cost_estimate=pl.CostEstimate(
            flops=flops,
            bytes_accessed=2 * pairs.size * 2 + 4 * peers * parts[0].size,
            transcendentals=blocks * queries * keys_all,
        ),
    )(me, pairs, *parts)


def exchange(x):
    return lax.all_to_all(x, "docs", split_axis=0, concat_axis=0, tiled=True)


def send(x, distance, peers):
    return lax.ppermute(x, "heads", [(i, (i + distance) % peers) for i in range(peers)])


def shards(queries, keys, values, out_grad, doc_keys, doc_values, owner_pick, doc_pick):
    relays = lax.axis_size("docs")
    peers = lax.axis_size("heads")
    me = lax.axis_index("heads").astype(jnp.int32).reshape(1)
    blocks, fan = owner_pick.shape
    docs, _, head_dim = doc_keys.shape
    wide = queries.shape[2] // peers
    narrow = keys.shape[2] // peers
    group = wide // head_dim

    def beside(array, distances, sign, into):
        sent = [send(parts[s], sign * s, peers) for s in distances]
        array, *sent = lax.optimization_barrier([array] + sent)
        into.update(zip(distances, sent))
        return array

    parts = split_heads(me, queries, out_grad, keys, values, peers)
    got = {0: parts[0]}
    slices = exchange(split_docs(doc_keys, doc_values, owner_pick, doc_pick, relays))
    slices = beside(slices, (1, 7), 1, got)
    pairs, table = gather_pairs(slices, blocks, fan)
    pairs = beside(exchange(pairs), (2, 6, 3, 5, 4), 1, got)

    parts = [got[s] for s in range(peers)]
    grads, *parts = attend(me, pairs, parts, group, head_dim, fan)

    back = {0: parts[0]}
    grads = beside(exchange(grads), (2, 6, 3, 5, 4), -1, back)
    doc_grads = exchange(sum_pairs(table, grads, docs + 1, fan))
    back.update((s, send(parts[s], -s, peers)) for s in (1, 7))
    doc_key_grad, doc_value_grad = join_docs(doc_grads)
    parts = [back[s] for s in range(peers)]
    attended, query_grad, key_grad, value_grad = join_heads(me, parts, wide, narrow)
    return (attended, query_grad, key_grad, value_grad, doc_key_grad, doc_value_grad)


def solution(mesh):
    tokens = P("docs", "heads", None)
    documents = P("docs", None, "heads")
    picks = P("docs", None)
    return jax.shard_map(
        shards,
        mesh=mesh,
        in_specs=(tokens,) * 4 + (documents,) * 2 + (picks,) * 2,
        out_specs=(tokens,) * 4 + (documents,) * 2,
        check_vma=False,
    )
```

```python
import functools
import math

import jax
import jax.numpy as jnp
from jax import lax
from jax.experimental import pallas as pl
from jax.experimental.pallas import tpu as pltpu
from jax.sharding import PartitionSpec as P

VMEM = 64 * 1024 * 1024
SLICE = 16
LOG2E = 1.4426950408889634


def vmem():
    return pl.BlockSpec(memory_space=pltpu.VMEM)


def smem():
    return pl.BlockSpec(memory_space=pltpu.SMEM)


def params(room):
    return pltpu.CompilerParams(vmem_limit_bytes=VMEM - room)


def split_docs(doc_keys, doc_values, owner_pick, doc_pick, peers):
    docs, length, head_dim = doc_keys.shape
    blocks, fan = owner_pick.shape
    half = peers // 2

    def kernel(key_ref, value_ref, owner_ref, pick_ref, out_ref):
        chosen = (owner_ref[...] * docs + pick_ref[...]).astype(jnp.float32)
        row = jnp.concatenate([chosen[b : b + 1] for b in range(blocks)], axis=1)
        row = jnp.pad(row, ((0, 0), (0, head_dim - blocks * fan)))
        chosen = jnp.broadcast_to(row, (SLICE, head_dim)).astype(jnp.bfloat16)
        for i in range(half):
            rows = slice(i * SLICE, (i + 1) * SLICE)
            out_ref[i, :docs] = key_ref[:, rows, :]
            out_ref[half + i, :docs] = value_ref[:, rows, :]
            out_ref[i, docs] = chosen
            out_ref[half + i, docs] = chosen

    return pl.pallas_call(
        kernel,
        out_shape=jax.ShapeDtypeStruct((peers, docs + 1, SLICE, head_dim), jnp.bfloat16),
        in_specs=[vmem()] * 4,
        out_specs=vmem(),
        compiler_params=params(131072),
    )(doc_keys, doc_values, owner_pick, doc_pick)


def join_docs(slices, steps=2):
    peers, docs, rows, head_dim = slices.shape
    half = peers // 2
    part = docs // steps
    shape = jax.ShapeDtypeStruct((docs, half * rows, head_dim), jnp.bfloat16)
    doc_spec = pl.BlockSpec((part, half * rows, head_dim), lambda i: (i, 0, 0))

    def kernel(in_ref, key_ref, value_ref):
        for i in range(half):
            at = slice(i * rows, (i + 1) * rows)
            key_ref[:, at, :] = in_ref[i]
            value_ref[:, at, :] = in_ref[half + i]

    return pl.pallas_call(
        kernel,
        out_shape=(shape, shape),
        grid=(steps,),
        in_specs=[pl.BlockSpec((peers, part, rows, head_dim), lambda i: (0, i, 0, 0))],
        out_specs=(doc_spec, doc_spec),
        compiler_params=params(33554432),
    )(slices)


def split_heads(me, queries, out_grad, keys, values, peers):
    blocks, rows, features = queries.shape
    wide = features // peers
    narrow = keys.shape[2] // peers
    width = 2 * wide + 2 * narrow

    def kernel(me_ref, q_ref, g_ref, k_ref, v_ref, *outs):
        for s in range(peers):
            head = lax.rem(me_ref[0] + s, peers)
            big = pl.ds(pl.multiple_of(head * wide, wide), wide)
            small = pl.ds(pl.multiple_of(head * narrow, narrow), narrow)
            outs[s][:, :, 0:wide] = q_ref[:, :, big]
            outs[s][:, :, wide : 2 * wide] = g_ref[:, :, big]
            outs[s][:, :, 2 * wide : 2 * wide + narrow] = k_ref[:, :, small]
            outs[s][:, :, 2 * wide + narrow : width] = v_ref[:, :, small]

    shape = jax.ShapeDtypeStruct((blocks, rows, width), jnp.bfloat16)
    return pl.pallas_call(
        kernel,
        out_shape=(shape,) * peers,
        in_specs=[smem()] + [vmem()] * 4,
        out_specs=(vmem(),) * peers,
        compiler_params=params(1500000),
    )(me, queries, out_grad, keys, values)


def join_heads(me, parts, wide, narrow):
    peers = len(parts)
    blocks, rows, width = parts[0].shape

    def kernel(me_ref, *refs):
        ins, (a_ref, q_ref, k_ref, v_ref) = refs[:peers], refs[peers:]
        for s in range(peers):
            head = lax.rem(me_ref[0] + s, peers)
            big = pl.ds(pl.multiple_of(head * wide, wide), wide)
            small = pl.ds(pl.multiple_of(head * narrow, narrow), narrow)
            a_ref[:, :, big] = ins[s][:, :, 0:wide]
            q_ref[:, :, big] = ins[s][:, :, wide : 2 * wide]
            k_ref[:, :, small] = ins[s][:, :, 2 * wide : 2 * wide + narrow]
            v_ref[:, :, small] = ins[s][:, :, 2 * wide + narrow : width]

    big_shape = jax.ShapeDtypeStruct((blocks, rows, peers * wide), jnp.bfloat16)
    small_shape = jax.ShapeDtypeStruct((blocks, rows, peers * narrow), jnp.bfloat16)
    return pl.pallas_call(
        kernel,
        out_shape=(big_shape, big_shape, small_shape, small_shape),
        in_specs=[smem()] + [vmem()] * peers,
        out_specs=(vmem(),) * 4,
        compiler_params=params(1500000),
    )(me, *parts)


def gather_pairs(slices, blocks, fan, steps=2):
    peers, kept, rows, head_dim = slices.shape
    docs = kept - 1
    shift = docs.bit_length() - 1
    part = peers // steps
    pairs = blocks * fan
    table_shape = (peers, head_dim)

    def kernel(in_ref, out_ref, table_ref, chosen_ref, sem):
        step = pl.program_id(0)
        flat_ref = in_ref.reshape(peers * kept, rows, head_dim)

        @pl.when(step == 0)
        def _():
            tile = in_ref[:, docs].astype(jnp.float32)
            table = tile[:, 0].astype(jnp.int32)
            table_ref[...] = table + lax.shift_right_logical(table, shift)
            copy = pltpu.make_async_copy(table_ref, chosen_ref, sem)
            copy.start()
            copy.wait()

        def body(i, _):
            q = step * part + i
            for p in range(0, pairs, fan):
                tiles = [flat_ref[chosen_ref[q, p + f]] for f in range(fan)]
                for f in range(fan):
                    out_ref[i, p + f] = tiles[f]
            return 0

        lax.fori_loop(0, part, body, 0)

    return pl.pallas_call(
        kernel,
        out_shape=(
            jax.ShapeDtypeStruct((peers, pairs, rows, head_dim), jnp.bfloat16),
            jax.ShapeDtypeStruct(table_shape, jnp.int32),
        ),
        grid=(steps,),
        in_specs=[pl.BlockSpec(slices.shape, lambda i: (0, 0, 0, 0))],
        out_specs=(
            pl.BlockSpec((part, pairs, rows, head_dim), lambda i: (i, 0, 0, 0)),
            pl.BlockSpec(table_shape, lambda i: (0, 0)),
        ),
        scratch_shapes=[
            pltpu.SMEM(table_shape, jnp.int32),
            pltpu.SemaphoreType.DMA,
        ],
        compiler_params=params(33554432),
    )(slices)


def sum_pairs(table, pairs, kept, fan, steps=2):
    peers, count, rows, head_dim = pairs.shape
    part = peers // steps
    out_shape = (peers, kept - 1, rows, head_dim)

    def kernel(chosen_ref, in_ref, out_ref, acc_ref):
        step = pl.program_id(0)

        @pl.when(step == 0)
        def _():
            acc_ref[...] = jnp.zeros_like(acc_ref)

        def body(i, _):
            q = step * part + i
            for p in range(0, count, fan):
                at = [chosen_ref[q, p + f] for f in range(fan)]
                sums = [
                    acc_ref[at[f]] + in_ref[i, p + f].astype(jnp.float32)
                    for f in range(fan)
                ]
                for f in range(fan):
                    acc_ref[at[f]] = sums[f]
            return 0

        lax.fori_loop(0, part, body, 0)

        @pl.when(step == steps - 1)
        def _():
            for i in range(peers):
                rounded = acc_ref[i * kept : i * kept + kept - 1]
                out_ref[i] = rounded.astype(jnp.bfloat16)

    return pl.pallas_call(
        kernel,
        out_shape=jax.ShapeDtypeStruct(out_shape, jnp.bfloat16),
        grid=(steps,),
        in_specs=[
            smem(),
            pl.BlockSpec((part, count, rows, head_dim), lambda i: (i, 0, 0, 0)),
        ],
        out_specs=pl.BlockSpec(out_shape, lambda i: (0, 0, 0, 0)),
        scratch_shapes=[pltpu.VMEM((peers * kept, rows, head_dim), jnp.float32)],
        compiler_params=params(33554432),
    )(table, pairs)


def attend_kernel(
    peers, rows, group, head_dim, me_ref, kv_ref, *refs
):
    ins, refs = refs[:peers], refs[peers:]
    dkv_ref, outs = refs[0], refs[1 : 1 + peers]
    k_all, v_all, k_t, v_t, q_n, q_t, g_n, g_t, s_t, p_t, ds_t = refs[1 + peers :]
    half, fan = kv_ref.shape[0] // 2, kv_ref.shape[1]
    doc_rows = half * fan * SLICE
    own = peers * rows
    keys_all = doc_rows + own
    wide = group * head_dim
    scaling = 1.0 / math.sqrt(head_dim)
    f32, bf16 = jnp.float32, jnp.bfloat16
    queries = group * own

    def dot(a, b):
        return jnp.dot(a, b, preferred_element_type=f32)

    k_all[:doc_rows] = kv_ref[:half].reshape(doc_rows, head_dim)
    v_all[:doc_rows] = kv_ref[half:].reshape(doc_rows, head_dim)
    for s in range(peers):
        at = slice(doc_rows + s * rows, doc_rows + (s + 1) * rows)
        k_all[at] = ins[s][0, :, 2 * wide : 2 * wide + head_dim]
        v_all[at] = ins[s][0, :, 2 * wide + head_dim : 2 * wide + 2 * head_dim]
        for g in range(group):
            to = slice(g * own + s * rows, g * own + (s + 1) * rows)
            q_n[to] = ins[s][0, :, g * head_dim : (g + 1) * head_dim]
            g_n[to] = ins[s][0, :, wide + g * head_dim : wide + (g + 1) * head_dim]
    k_t[...] = k_all[...].T
    v_t[:head_dim] = v_all[...].T
    v_t[head_dim:] = jnp.ones((v_t.shape[0] - head_dim, keys_all), bf16)
    q_t[...] = q_n[...].T
    g_t[...] = g_n[...].T

    def place(index):
        source = lax.rem(me_ref[0] + peers - index // rows, peers)
        return source * rows + lax.rem(index, rows)

    chunk = 2 * own
    key_place = place(lax.broadcasted_iota(jnp.int32, (own, chunk), 0))
    query_place = place(lax.rem(lax.broadcasted_iota(jnp.int32, (own, chunk), 1), own))
    hidden = key_place > query_place
    tiles = [slice(t, min(t + 256, doc_rows)) for t in range(0, doc_rows, 256)]
    tiles.append(slice(doc_rows, keys_all))

    def rows_max(x):
        return jnp.max(x.reshape(x.shape[0] // 8, 8, chunk), axis=0)

    def score(c, buf):
        q_c = q_t[:, c * chunk : (c + 1) * chunk]
        top = None
        for t in tiles:
            x = dot(k_all[t], q_c)
            if t.start == doc_rows:
                x = jnp.where(hidden, -jnp.inf, x)
            buf[t] = x
            m = rows_max(x)
            top = m if top is None else jnp.maximum(top, m)
        return jnp.max(top, axis=0, keepdims=True)

    def finish(c, o):
        at = slice(c * chunk, (c + 1) * chunk)
        g_c = g_t[:, at].astype(f32)
        inverse = 1.0 / o[head_dim : head_dim + 1]
        attended = (o[:head_dim] * inverse).astype(bf16)
        row_dot = jnp.sum(g_c * attended.astype(f32), axis=0, keepdims=True)
        g_n[at] = (g_c * inverse).astype(bf16).T
        return attended, row_dot, inverse * scaling

    def put(c, x, base):
        x = x.T
        for g in range(chunk // own):
            lanes = slice(base + (c * (chunk // own) + g) * head_dim, base + (c * (chunk // own) + g + 1) * head_dim)
            for s in range(peers):
                outs[s][0, :, lanes] = x[g * own + s * rows : g * own + (s + 1) * rows]

    tops = [score(0, s_t.at[0])]
    count = queries // chunk
    for c in range(count):
        at = slice(c * chunk, (c + 1) * chunk)
        cur, nxt = s_t.at[c % 2], s_t.at[(c + 1) % 2]
        m = None
        q_c = q_t[:, (c + 1) * chunk : (c + 2) * chunk] if c + 1 < count else None
        for t in tiles:
            p_t[t, at] = jnp.exp2((cur[t] - tops[c]) * (scaling * LOG2E)).astype(bf16)
            if q_c is not None:
                x = dot(k_all[t], q_c)
                if t.start == doc_rows:
                    x = jnp.where(hidden, -jnp.inf, x)
                nxt[t] = x
                y = rows_max(x)
                m = y if m is None else jnp.maximum(m, y)
        if m is not None:
            tops.append(jnp.max(m, axis=0, keepdims=True))
        attended, row_dot, factor = finish(c, dot(v_t[...], p_t[:, at]))
        g_c = g_t[:, at]
        for t in tiles:
            dp = dot(v_all[t], g_c)
            ds_t[t, at] = (p_t[t, at].astype(f32) * ((dp - row_dot) * factor)).astype(bf16)
        put(c, attended, 0)
        put(c, dot(k_t[...], ds_t[:, at]).astype(bf16), wide)

    dv = dot(p_t[...], g_n[...]).astype(bf16)
    dk = dot(ds_t[...], q_n[...]).astype(bf16)
    dkv_ref[:half] = dk[:doc_rows].reshape(half, fan, SLICE, head_dim)
    dkv_ref[half:] = dv[:doc_rows].reshape(half, fan, SLICE, head_dim)
    for s in range(peers):
        at = slice(doc_rows + s * rows, doc_rows + (s + 1) * rows)
        outs[s][0, :, 2 * wide : 2 * wide + head_dim] = dk[at]
        outs[s][0, :, 2 * wide + head_dim : 2 * wide + 2 * head_dim] = dv[at]


def attend(me, pairs, parts, group, head_dim, fan):
    peers = len(parts)
    _, rows, width = parts[0].shape
    relays = pairs.shape[0]
    blocks = pairs.shape[1] // fan
    own = peers * rows
    queries = group * own
    keys_all = relays // 2 * fan * SLICE + own
    bf16, f32 = jnp.bfloat16, jnp.float32
    part_spec = pl.BlockSpec((1, rows, width), lambda b: (b, 0, 0))
    pair_spec = pl.BlockSpec((relays, fan, SLICE, head_dim), lambda b: (0, b, 0, 0))
    part_shape = jax.ShapeDtypeStruct(parts[0].shape, bf16)
    flops = 12 * blocks * queries * keys_all * head_dim
    return pl.pallas_call(
        functools.partial(attend_kernel, peers, rows, group, head_dim),
        out_shape=(jax.ShapeDtypeStruct(pairs.shape, bf16),) + (part_shape,) * peers,
        grid=(blocks,),
        in_specs=[smem(), pair_spec] + [part_spec] * peers,
        out_specs=(pair_spec,) + (part_spec,) * peers,
        scratch_shapes=[
            pltpu.VMEM((keys_all, head_dim), bf16),
            pltpu.VMEM((keys_all, head_dim), bf16),
            pltpu.VMEM((head_dim, keys_all), bf16),
            pltpu.VMEM((head_dim + 16, keys_all), bf16),
            pltpu.VMEM((queries, head_dim), bf16),
            pltpu.VMEM((head_dim, queries), bf16),
            pltpu.VMEM((queries, head_dim), bf16),
            pltpu.VMEM((head_dim, queries), bf16),
            pltpu.VMEM((2, keys_all, 2 * own), f32),
            pltpu.VMEM((keys_all, queries), bf16),
            pltpu.VMEM((keys_all, queries), bf16),
        ],
        compiler_params=params(131072),
        cost_estimate=pl.CostEstimate(
            flops=flops,
            bytes_accessed=2 * pairs.size * 2 + 4 * peers * parts[0].size,
            transcendentals=blocks * queries * keys_all,
        ),
    )(me, pairs, *parts)


def exchange(x):
    return lax.all_to_all(x, "docs", split_axis=0, concat_axis=0, tiled=True)


def send(x, distance, peers):
    return lax.ppermute(x, "heads", [(i, (i + distance) % peers) for i in range(peers)])


def shards(queries, keys, values, out_grad, doc_keys, doc_values, owner_pick, doc_pick):
    relays = lax.axis_size("docs")
    peers = lax.axis_size("heads")
    me = lax.axis_index("heads").astype(jnp.int32).reshape(1)
    blocks, fan = owner_pick.shape
    docs, _, head_dim = doc_keys.shape
    wide = queries.shape[2] // peers
    narrow = keys.shape[2] // peers
    group = wide // head_dim

    def beside(array, distances, sign, into):
        sent = [send(parts[s], sign * s, peers) for s in distances]
        array, *sent = lax.optimization_barrier([array] + sent)
        into.update(zip(distances, sent))
        return array

    parts = split_heads(me, queries, out_grad, keys, values, peers)
    got = {0: parts[0]}
    slices = exchange(split_docs(doc_keys, doc_values, owner_pick, doc_pick, relays))
    slices = beside(slices, (1, 7), 1, got)
    pairs, table = gather_pairs(slices, blocks, fan)
    pairs = beside(exchange(pairs), (2, 6, 3, 5, 4), 1, got)

    parts = [got[s] for s in range(peers)]
    grads, *parts = attend(me, pairs, parts, group, head_dim, fan)

    back = {0: parts[0]}
    grads = beside(exchange(grads), (2, 6, 3, 5, 4), -1, back)
    doc_grads = exchange(sum_pairs(table, grads, docs + 1, fan))
    back.update((s, send(parts[s], -s, peers)) for s in (1, 7))
    doc_key_grad, doc_value_grad = join_docs(doc_grads)
    parts = [back[s] for s in range(peers)]
    attended, query_grad, key_grad, value_grad = join_heads(me, parts, wide, narrow)
    return (attended, query_grad, key_grad, value_grad, doc_key_grad, doc_value_grad)


def solution(mesh):
    tokens = P("docs", "heads", None)
    documents = P("docs", None, "heads")
    picks = P("docs", None)
    return jax.shard_map(
        shards,
        mesh=mesh,
        in_specs=(tokens,) * 4 + (documents,) * 2 + (picks,) * 2,
        out_specs=(tokens,) * 4 + (documents,) * 2,
        check_vma=False,
    )
```

```python
import functools
import math

import jax
import jax.numpy as jnp
from jax import lax
from jax.experimental import pallas as pl
from jax.experimental.pallas import tpu as pltpu
from jax.sharding import PartitionSpec as P

VMEM = 64 * 1024 * 1024
SLICE = 16
LOG2E = 1.4426950408889634


def vmem():
    return pl.BlockSpec(memory_space=pltpu.VMEM)


def smem():
    return pl.BlockSpec(memory_space=pltpu.SMEM)


def params(room):
    return pltpu.CompilerParams(vmem_limit_bytes=VMEM - room)


def split_docs(doc_keys, doc_values, owner_pick, doc_pick, peers):
    docs, length, head_dim = doc_keys.shape
    blocks, fan = owner_pick.shape
    half = peers // 2

    def kernel(key_ref, value_ref, owner_ref, pick_ref, out_ref):
        chosen = (owner_ref[...] * docs + pick_ref[...]).astype(jnp.float32)
        row = jnp.concatenate([chosen[b : b + 1] for b in range(blocks)], axis=1)
        row = jnp.pad(row, ((0, 0), (0, head_dim - blocks * fan)))
        chosen = jnp.broadcast_to(row, (SLICE, head_dim)).astype(jnp.bfloat16)
        for i in range(half):
            rows = slice(i * SLICE, (i + 1) * SLICE)
            out_ref[i, :docs] = key_ref[:, rows, :]
            out_ref[half + i, :docs] = value_ref[:, rows, :]
            out_ref[i, docs] = chosen
            out_ref[half + i, docs] = chosen

    return pl.pallas_call(
        kernel,
        out_shape=jax.ShapeDtypeStruct((peers, docs + 1, SLICE, head_dim), jnp.bfloat16),
        in_specs=[vmem()] * 4,
        out_specs=vmem(),
        compiler_params=params(131072),
    )(doc_keys, doc_values, owner_pick, doc_pick)


def join_docs(slices, steps=2):
    peers, docs, rows, head_dim = slices.shape
    half = peers // 2
    part = docs // steps
    shape = jax.ShapeDtypeStruct((docs, half * rows, head_dim), jnp.bfloat16)
    doc_spec = pl.BlockSpec((part, half * rows, head_dim), lambda i: (i, 0, 0))

    def kernel(in_ref, key_ref, value_ref):
        for i in range(half):
            at = slice(i * rows, (i + 1) * rows)
            key_ref[:, at, :] = in_ref[i]
            value_ref[:, at, :] = in_ref[half + i]

    return pl.pallas_call(
        kernel,
        out_shape=(shape, shape),
        grid=(steps,),
        in_specs=[pl.BlockSpec((peers, part, rows, head_dim), lambda i: (0, i, 0, 0))],
        out_specs=(doc_spec, doc_spec),
        compiler_params=params(33554432),
    )(slices)


def split_heads(me, queries, out_grad, keys, values, peers):
    blocks, rows, features = queries.shape
    wide = features // peers
    narrow = keys.shape[2] // peers
    width = 2 * wide + 2 * narrow

    def kernel(me_ref, q_ref, g_ref, k_ref, v_ref, *outs):
        for s in range(peers):
            head = lax.rem(me_ref[0] + s, peers)
            big = pl.ds(pl.multiple_of(head * wide, wide), wide)
            small = pl.ds(pl.multiple_of(head * narrow, narrow), narrow)
            outs[s][:, :, 0:wide] = q_ref[:, :, big]
            outs[s][:, :, wide : 2 * wide] = g_ref[:, :, big]
            outs[s][:, :, 2 * wide : 2 * wide + narrow] = k_ref[:, :, small]
            outs[s][:, :, 2 * wide + narrow : width] = v_ref[:, :, small]

    shape = jax.ShapeDtypeStruct((blocks, rows, width), jnp.bfloat16)
    return pl.pallas_call(
        kernel,
        out_shape=(shape,) * peers,
        in_specs=[smem()] + [vmem()] * 4,
        out_specs=(vmem(),) * peers,
        compiler_params=params(1500000),
    )(me, queries, out_grad, keys, values)


def join_heads(me, parts, wide, narrow):
    peers = len(parts)
    blocks, rows, width = parts[0].shape

    def kernel(me_ref, *refs):
        ins, (a_ref, q_ref, k_ref, v_ref) = refs[:peers], refs[peers:]
        for s in range(peers):
            head = lax.rem(me_ref[0] + s, peers)
            big = pl.ds(pl.multiple_of(head * wide, wide), wide)
            small = pl.ds(pl.multiple_of(head * narrow, narrow), narrow)
            a_ref[:, :, big] = ins[s][:, :, 0:wide]
            q_ref[:, :, big] = ins[s][:, :, wide : 2 * wide]
            k_ref[:, :, small] = ins[s][:, :, 2 * wide : 2 * wide + narrow]
            v_ref[:, :, small] = ins[s][:, :, 2 * wide + narrow : width]

    big_shape = jax.ShapeDtypeStruct((blocks, rows, peers * wide), jnp.bfloat16)
    small_shape = jax.ShapeDtypeStruct((blocks, rows, peers * narrow), jnp.bfloat16)
    return pl.pallas_call(
        kernel,
        out_shape=(big_shape, big_shape, small_shape, small_shape),
        in_specs=[smem()] + [vmem()] * peers,
        out_specs=(vmem(),) * 4,
        compiler_params=params(1500000),
    )(me, *parts)


def gather_pairs(slices, blocks, fan, steps=2):
    peers, kept, rows, head_dim = slices.shape
    docs = kept - 1
    shift = docs.bit_length() - 1
    part = peers // steps
    pairs = blocks * fan
    table_shape = (peers, head_dim)

    def kernel(in_ref, out_ref, table_ref, chosen_ref, sem):
        step = pl.program_id(0)
        flat_ref = in_ref.reshape(peers * kept, rows, head_dim)

        @pl.when(step == 0)
        def _():
            tile = in_ref[:, docs].astype(jnp.float32)
            table = tile[:, 0].astype(jnp.int32)
            table_ref[...] = table + lax.shift_right_logical(table, shift)
            copy = pltpu.make_async_copy(table_ref, chosen_ref, sem)
            copy.start()
            copy.wait()

        def body(i, _):
            q = step * part + i
            for p in range(0, pairs, fan):
                tiles = [flat_ref[chosen_ref[q, p + f]] for f in range(fan)]
                for f in range(fan):
                    out_ref[i, p + f] = tiles[f]
            return 0

        lax.fori_loop(0, part, body, 0)

    return pl.pallas_call(
        kernel,
        out_shape=(
            jax.ShapeDtypeStruct((peers, pairs, rows, head_dim), jnp.bfloat16),
            jax.ShapeDtypeStruct(table_shape, jnp.int32),
        ),
        grid=(steps,),
        in_specs=[pl.BlockSpec(slices.shape, lambda i: (0, 0, 0, 0))],
        out_specs=(
            pl.BlockSpec((part, pairs, rows, head_dim), lambda i: (i, 0, 0, 0)),
            pl.BlockSpec(table_shape, lambda i: (0, 0)),
        ),
        scratch_shapes=[
            pltpu.SMEM(table_shape, jnp.int32),
            pltpu.SemaphoreType.DMA,
        ],
        compiler_params=params(4000000),
    )(slices)


def sum_pairs(table, pairs, kept, fan, steps=2):
    peers, count, rows, head_dim = pairs.shape
    part = peers // steps
    out_shape = (peers, kept - 1, rows, head_dim)

    def kernel(chosen_ref, in_ref, out_ref, acc_ref):
        step = pl.program_id(0)

        @pl.when(step == 0)
        def _():
            acc_ref[...] = jnp.zeros_like(acc_ref)

        def body(i, _):
            q = step * part + i
            for p in range(0, count, fan):
                at = [chosen_ref[q, p + f] for f in range(fan)]
                sums = [
                    acc_ref[at[f]] + in_ref[i, p + f].astype(jnp.float32)
                    for f in range(fan)
                ]
                for f in range(fan):
                    acc_ref[at[f]] = sums[f]
            return 0

        lax.fori_loop(0, part, body, 0)

        @pl.when(step == steps - 1)
        def _():
            for i in range(peers):
                rounded = acc_ref[i * kept : i * kept + kept - 1]
                out_ref[i] = rounded.astype(jnp.bfloat16)

    return pl.pallas_call(
        kernel,
        out_shape=jax.ShapeDtypeStruct(out_shape, jnp.bfloat16),
        grid=(steps,),
        in_specs=[
            smem(),
            pl.BlockSpec((part, count, rows, head_dim), lambda i: (i, 0, 0, 0)),
        ],
        out_specs=pl.BlockSpec(out_shape, lambda i: (0, 0, 0, 0)),
        scratch_shapes=[pltpu.VMEM((peers * kept, rows, head_dim), jnp.float32)],
        compiler_params=params(4000000),
    )(table, pairs)


def attend_kernel(
    peers, rows, group, head_dim, me_ref, kv_ref, *refs
):
    ins, refs = refs[:peers], refs[peers:]
    dkv_ref, outs = refs[0], refs[1 : 1 + peers]
    k_all, v_all, k_t, v_t, q_n, q_t, g_n, g_t, s_t, p_t, ds_t = refs[1 + peers :]
    half, fan = kv_ref.shape[0] // 2, kv_ref.shape[1]
    doc_rows = half * fan * SLICE
    own = peers * rows
    keys_all = doc_rows + own
    wide = group * head_dim
    scaling = 1.0 / math.sqrt(head_dim)
    f32, bf16 = jnp.float32, jnp.bfloat16
    queries = group * own

    def dot(a, b):
        return jnp.dot(a, b, preferred_element_type=f32)

    k_all[:doc_rows] = kv_ref[:half].reshape(doc_rows, head_dim)
    v_all[:doc_rows] = kv_ref[half:].reshape(doc_rows, head_dim)
    for s in range(peers):
        at = slice(doc_rows + s * rows, doc_rows + (s + 1) * rows)
        k_all[at] = ins[s][0, :, 2 * wide : 2 * wide + head_dim]
        v_all[at] = ins[s][0, :, 2 * wide + head_dim : 2 * wide + 2 * head_dim]
        for g in range(group):
            to = slice(g * own + s * rows, g * own + (s + 1) * rows)
            q_n[to] = ins[s][0, :, g * head_dim : (g + 1) * head_dim]
            g_n[to] = ins[s][0, :, wide + g * head_dim : wide + (g + 1) * head_dim]
    k_t[...] = k_all[...].T
    v_t[:head_dim] = v_all[...].T
    v_t[head_dim:] = jnp.ones((v_t.shape[0] - head_dim, keys_all), bf16)
    q_t[...] = q_n[...].T
    g_t[...] = g_n[...].T

    def place(index):
        source = lax.rem(me_ref[0] + peers - index // rows, peers)
        return source * rows + lax.rem(index, rows)

    chunk = 2 * own
    key_place = place(lax.broadcasted_iota(jnp.int32, (own, chunk), 0))
    query_place = place(lax.rem(lax.broadcasted_iota(jnp.int32, (own, chunk), 1), own))
    hidden = key_place > query_place
    tiles = [slice(t, min(t + 256, doc_rows)) for t in range(0, doc_rows, 256)]
    tiles.append(slice(doc_rows, keys_all))

    def rows_max(x):
        return jnp.max(x.reshape(x.shape[0] // 8, 8, chunk), axis=0)

    def score(c, buf):
        q_c = q_t[:, c * chunk : (c + 1) * chunk]
        top = None
        for t in tiles:
            x = dot(k_all[t], q_c)
            if t.start == doc_rows:
                x = jnp.where(hidden, -jnp.inf, x)
            buf[t] = x
            m = rows_max(x)
            top = m if top is None else jnp.maximum(top, m)
        return jnp.max(top, axis=0, keepdims=True)

    def finish(c, o):
        at = slice(c * chunk, (c + 1) * chunk)
        g_c = g_t[:, at].astype(f32)
        inverse = 1.0 / o[head_dim : head_dim + 1]
        attended = (o[:head_dim] * inverse).astype(bf16)
        row_dot = jnp.sum(g_c * attended.astype(f32), axis=0, keepdims=True)
        g_n[at] = (g_c * inverse).astype(bf16).T
        return attended, row_dot, inverse * scaling

    def put(c, x, base):
        x = x.T
        for g in range(chunk // own):
            lanes = slice(base + (c * (chunk // own) + g) * head_dim, base + (c * (chunk // own) + g + 1) * head_dim)
            for s in range(peers):
                outs[s][0, :, lanes] = x[g * own + s * rows : g * own + (s + 1) * rows]

    tops = [score(0, s_t.at[0])]
    count = queries // chunk
    for c in range(count):
        at = slice(c * chunk, (c + 1) * chunk)
        cur, nxt = s_t.at[c % 2], s_t.at[(c + 1) % 2]
        m = None
        q_c = q_t[:, (c + 1) * chunk : (c + 2) * chunk] if c + 1 < count else None
        for t in tiles:
            p_t[t, at] = jnp.exp2((cur[t] - tops[c]) * (scaling * LOG2E)).astype(bf16)
            if q_c is not None:
                x = dot(k_all[t], q_c)
                if t.start == doc_rows:
                    x = jnp.where(hidden, -jnp.inf, x)
                nxt[t] = x
                y = rows_max(x)
                m = y if m is None else jnp.maximum(m, y)
        if m is not None:
            tops.append(jnp.max(m, axis=0, keepdims=True))
        attended, row_dot, factor = finish(c, dot(v_t[...], p_t[:, at]))
        g_c = g_t[:, at]
        for t in tiles:
            dp = dot(v_all[t], g_c)
            ds_t[t, at] = (p_t[t, at].astype(f32) * ((dp - row_dot) * factor)).astype(bf16)
        put(c, attended, 0)
        put(c, dot(k_t[...], ds_t[:, at]).astype(bf16), wide)

    dv = dot(p_t[...], g_n[...]).astype(bf16)
    dk = dot(ds_t[...], q_n[...]).astype(bf16)
    dkv_ref[:half] = dk[:doc_rows].reshape(half, fan, SLICE, head_dim)
    dkv_ref[half:] = dv[:doc_rows].reshape(half, fan, SLICE, head_dim)
    for s in range(peers):
        at = slice(doc_rows + s * rows, doc_rows + (s + 1) * rows)
        outs[s][0, :, 2 * wide : 2 * wide + head_dim] = dk[at]
        outs[s][0, :, 2 * wide + head_dim : 2 * wide + 2 * head_dim] = dv[at]


def attend(me, pairs, parts, group, head_dim, fan):
    peers = len(parts)
    _, rows, width = parts[0].shape
    relays = pairs.shape[0]
    blocks = pairs.shape[1] // fan
    own = peers * rows
    queries = group * own
    keys_all = relays // 2 * fan * SLICE + own
    bf16, f32 = jnp.bfloat16, jnp.float32
    part_spec = pl.BlockSpec((1, rows, width), lambda b: (b, 0, 0))
    pair_spec = pl.BlockSpec((relays, fan, SLICE, head_dim), lambda b: (0, b, 0, 0))
    part_shape = jax.ShapeDtypeStruct(parts[0].shape, bf16)
    flops = 12 * blocks * queries * keys_all * head_dim
    return pl.pallas_call(
        functools.partial(attend_kernel, peers, rows, group, head_dim),
        out_shape=(jax.ShapeDtypeStruct(pairs.shape, bf16),) + (part_shape,) * peers,
        grid=(blocks,),
        in_specs=[smem(), pair_spec] + [part_spec] * peers,
        out_specs=(pair_spec,) + (part_spec,) * peers,
        scratch_shapes=[
            pltpu.VMEM((keys_all, head_dim), bf16),
            pltpu.VMEM((keys_all, head_dim), bf16),
            pltpu.VMEM((head_dim, keys_all), bf16),
            pltpu.VMEM((head_dim + 16, keys_all), bf16),
            pltpu.VMEM((queries, head_dim), bf16),
            pltpu.VMEM((head_dim, queries), bf16),
            pltpu.VMEM((queries, head_dim), bf16),
            pltpu.VMEM((head_dim, queries), bf16),
            pltpu.VMEM((2, keys_all, 2 * own), f32),
            pltpu.VMEM((keys_all, queries), bf16),
            pltpu.VMEM((keys_all, queries), bf16),
        ],
        compiler_params=params(131072),
        cost_estimate=pl.CostEstimate(
            flops=flops,
            bytes_accessed=2 * pairs.size * 2 + 4 * peers * parts[0].size,
            transcendentals=blocks * queries * keys_all,
        ),
    )(me, pairs, *parts)


def exchange(x):
    return lax.all_to_all(x, "docs", split_axis=0, concat_axis=0, tiled=True)


def send(x, distance, peers):
    return lax.ppermute(x, "heads", [(i, (i + distance) % peers) for i in range(peers)])


def shards(queries, keys, values, out_grad, doc_keys, doc_values, owner_pick, doc_pick):
    relays = lax.axis_size("docs")
    peers = lax.axis_size("heads")
    me = lax.axis_index("heads").astype(jnp.int32).reshape(1)
    blocks, fan = owner_pick.shape
    docs, _, head_dim = doc_keys.shape
    wide = queries.shape[2] // peers
    narrow = keys.shape[2] // peers
    group = wide // head_dim

    def beside(array, distances, sign, into):
        sent = [send(parts[s], sign * s, peers) for s in distances]
        array, *sent = lax.optimization_barrier([array] + sent)
        into.update(zip(distances, sent))
        return array

    parts = split_heads(me, queries, out_grad, keys, values, peers)
    got = {0: parts[0]}
    slices = exchange(split_docs(doc_keys, doc_values, owner_pick, doc_pick, relays))
    slices = beside(slices, (1, 7), 1, got)
    pairs, table = gather_pairs(slices, blocks, fan)
    pairs = beside(exchange(pairs), (2, 6, 3, 5, 4), 1, got)

    parts = [got[s] for s in range(peers)]
    grads, *parts = attend(me, pairs, parts, group, head_dim, fan)

    back = {0: parts[0]}
    grads = beside(exchange(grads), (2, 6, 3, 5, 4), -1, back)
    doc_grads = exchange(sum_pairs(table, grads, docs + 1, fan))
    back.update((s, send(parts[s], -s, peers)) for s in (1, 7))
    doc_key_grad, doc_value_grad = join_docs(doc_grads)
    parts = [back[s] for s in range(peers)]
    attended, query_grad, key_grad, value_grad = join_heads(me, parts, wide, narrow)
    return (attended, query_grad, key_grad, value_grad, doc_key_grad, doc_value_grad)


def solution(mesh):
    tokens = P("docs", "heads", None)
    documents = P("docs", None, "heads")
    picks = P("docs", None)
    return jax.shard_map(
        shards,
        mesh=mesh,
        in_specs=(tokens,) * 4 + (documents,) * 2 + (picks,) * 2,
        out_specs=(tokens,) * 4 + (documents,) * 2,
        check_vma=False,
    )
```
